32 devices in a mesh: dp: 8 (over y, x, core), tensor: 4 (over z).
Axes of the slice: x: 2, y: 2, z: 4, core: 2. Of those that a mesh axis runs over, the one named last changes fastest.
Arguments:
- context: bfloat16 [7680, 6144], P('dp', 'tensor'), may hold values from -6 to 6
- out_grad: bfloat16 [7680, 32], P(('dp', 'tensor')), may hold values from -0.0625 to 0.0625
- owner_table: int32 [8], replicated, may hold values from 0 to 7, each once
- step_count: int32 [1], replicated, may hold values from 1 to 19
- master: float32 [8, 4, 6144], P('dp', None, 'tensor'), may hold values from -0.3125 to 0.3125
- first_moment: float32 [8, 4, 6144], P('dp', None, 'tensor'), may hold values from -6 to 6
- second_moment: float32 [8, 4, 6144], P('dp', None, 'tensor'), may hold values from 0.1 to 4
Outputs:
- new_master: float32 [8, 4, 6144], P('dp', None, 'tensor')
- new_first: float32 [8, 4, 6144], P('dp', None, 'tensor')
- new_second: float32 [8, 4, 6144], P('dp', None, 'tensor')
- new_weight: bfloat16 [32, 6144], P(None, 'tensor')
The draws below stay inside these ranges and needn't reach their ends.
Inputs may be any that keep to these rules, and one draw needn't show every extreme that they name: `owner_table`: each state row holds exactly one bucket.
All inputs are finite; a program needn't handle non-finite values.
Results may differ from the reference program's by a relative error of at most 0.0004.
Values may be sent and summed in bfloat16 or wider, within the bound.
A program may use at most 64 MiB of HBM per device.

```python
import math
import jax
import jax.numpy as jnp

BW = 4
ROWS = 6144
TOKENS = 7680
NB = 8
WIN = 32


def levels(own_key, dims, shards, low, largest):
    def one(axis_at, shards_of):
        steps = jax.random.uniform(jax.random.fold_in(jax.random.fold_in(own_key, 6), axis_at), (shards_of,), jnp.float32, low / len(shards), largest / len(shards))
        return jnp.repeat(jnp.exp(steps), dims[axis_at] // shards_of).reshape((-1,) + (1,) * (len(dims) - axis_at - 1))

    factor_of = one(*shards[0])
    for cut in shards[1:]:
        factor_of = factor_of * one(*cut)
    return factor_of


def centred(key, shape, deviation, bound, pieces=(), kind=jnp.bfloat16):
    loudness = levels(key, shape, pieces, -0.22, 0.18) if pieces else 1.0
    array = jax.random.normal(key, shape, jnp.float32) * deviation * loudness
    return jnp.minimum(jnp.maximum(array, -bound), bound).astype(kind)


def setup_inputs(seed: int = 0) -> dict:
    keys = jax.random.split(jax.random.key(seed), 8)
    context = centred(keys[0], (TOKENS, ROWS), 1.0, 6.0, ((0, 8), (1, 4)))
    out_grad = centred(keys[1], (TOKENS, WIN), TOKENS ** -0.5, 0.0625, ((0, 32),))
    owner_table = jax.random.permutation(keys[2], NB).astype(jnp.int32)
    step_count = jax.random.randint(keys[3], (1,), 1, 20).astype(jnp.int32)
    master = centred(keys[4], (NB, BW, ROWS), 0.02, 0.3125, ((0, 8), (2, 4)), jnp.float32)
    first_moment = centred(keys[5], (NB, BW, ROWS), 1.0, 6.0, ((0, 8), (2, 4)), jnp.float32)
    second_moment = jnp.clip(jnp.exp(math.log(4.0) - 3.6888794 * jax.random.uniform(keys[6], (NB, BW, ROWS), jnp.float32) ** levels(keys[6], (NB, BW, ROWS), ((0, 8), (2, 4)), -0.2, 0.2)), 0.1, 4.0)
    return {"context": context, "out_grad": out_grad, "owner_table": owner_table, "step_count": step_count, "master": master, "first_moment": first_moment, "second_moment": second_moment}


def reference(context, out_grad, owner_table, step_count, master, first_moment, second_moment):
    grad = jnp.dot(out_grad.T, context, preferred_element_type=jnp.float32)
    blocks = grad.reshape(NB, BW, ROWS)
    order = jnp.zeros((NB,), jnp.int32).at[owner_table].set(jnp.arange(NB, dtype=jnp.int32))
    owned = jnp.take(blocks, order, axis=0)
    new_first = 0.9 * first_moment + 0.1 * owned
    new_second = 0.95 * second_moment + 0.05 * owned * owned
    steps = step_count[0].astype(jnp.float32)
    corr_one = 1.0 - jnp.exp(steps * math.log(0.9))
    corr_two = 1.0 - jnp.exp(steps * math.log(0.95))
    update = new_first / corr_one / (jnp.sqrt(new_second / corr_two) + 1e-08)
    new_master = master - 0.01 * (update + 0.01 * master)
    fresh = new_master.astype(jnp.bfloat16)
    new_weight = jnp.take(fresh, owner_table, axis=0).reshape(WIN, ROWS)
    return (new_master, new_first, new_second, new_weight)
```

```python
import functools
import math

import jax
import jax.numpy as jnp
from jax import lax
from jax.experimental import pallas as pl
from jax.experimental.pallas import tpu as pltpu
from jax.sharding import PartitionSpec as P

F32 = jnp.float32
BF16 = jnp.bfloat16


def each(low, high, body):
    if high - low <= 16:
        for at in range(low, high):
            body(at)
    else:
        lax.fori_loop(low, high, lambda at, none: (body(at), none)[1], None)


def kernel(
    owners, ranks, buckets, width,
    table, step, og_hbm, ctx_hbm, master_hbm, first_hbm, second_hbm,
    out_master, out_first, out_second, out_weight,
    og_own, og_all, ctx, acc, stage, parts, state, fresh, rows, weight,
    og_own_sem, ctx_sem, state_sem, out_sem,
    og_send, og_recv, part_send, part_recv, row_send, row_recv,
):
    me = lax.axis_index("dp")
    rank = lax.axis_index("tensor")
    window, tokens = og_own.shape
    columns = ctx.shape[2]
    groups = rows.shape[1] // width
    span = columns // groups

    barrier = pltpu.get_barrier_semaphore()

    def greet_rank(k):
        pl.semaphore_signal(barrier, inc=1, device_id={"tensor": lax.rem(rank + k, ranks)})

    def greet_owner(k):
        pl.semaphore_signal(barrier, inc=1, device_id={"dp": lax.rem(me + k, owners)})

    each(1, ranks, greet_rank)
    each(1, owners, greet_owner)

    own_copy = pltpu.make_async_copy(og_hbm, og_own, og_own_sem)
    own_copy.start()

    def ctx_copy(k):
        at = lax.rem(rank + k, ranks)
        first = pl.multiple_of(at * tokens, 16)
        return pltpu.make_async_copy(
            ctx_hbm.at[pl.ds(first, tokens), :], ctx.at[at], ctx_sem.at[at]
        )

    for k in range(ranks):
        ctx_copy(k).start()
    state_copies = [
        pltpu.make_async_copy(source.at[0], state.at[i], state_sem.at[i])
        for i, source in enumerate((master_hbm, first_hbm, second_hbm))
    ]
    for copy in state_copies:
        copy.start()

    lane_bucket = lax.broadcasted_iota(jnp.int32, (1, window), 1) // width
    owner_of = jnp.zeros((1, window), jnp.int32)
    for b in range(buckets):
        owner_of = jnp.where(lane_bucket == b, table[b], owner_of)
    down = lax.broadcasted_iota(jnp.int32, (window, window), 0)
    across = lax.broadcasted_iota(jnp.int32, (window, window), 1)
    chosen = jnp.logical_and(owner_of == down // width, down % width == across % width)
    pick = jnp.where(chosen, 1.0, 0.0).astype(BF16)

    own_copy.wait()
    og_all[rank] = jnp.dot(pick, og_own[...], preferred_element_type=F32).astype(BF16)

    pl.semaphore_wait(barrier, ranks + owners - 2)

    def og_copy(k):
        peer = lax.rem(rank + k, ranks)
        return pltpu.make_async_remote_copy(
            src_ref=og_all.at[rank],
            dst_ref=og_all.at[rank],
            send_sem=og_send.at[k],
            recv_sem=og_recv.at[k],
            device_id={"tensor": peer},
        )

    def og_arrival(k):
        source = lax.rem(rank + ranks - k, ranks)
        return pltpu.make_async_remote_copy(
            src_ref=og_all.at[source],
            dst_ref=og_all.at[source],
            send_sem=og_send.at[k],
            recv_sem=og_recv.at[k],
            device_id={"tensor": source},
        )

    for k in range(1, ranks):
        og_copy(k).start()

    block = min(window, 8 * width)
    for i in range(ranks):
        at = lax.rem(rank + ranks - i, ranks)
        if i:
            og_arrival(i).wait_recv()
        ctx_copy((ranks - i) % ranks).wait()

        def multiply(m, i=i, at=at):
            here = pl.ds(m * block, block)
            value = jnp.dot(og_all[at, here, :], ctx[at], preferred_element_type=F32)
            if i:
                value = acc[here, :] + value
            if i < ranks - 1:
                acc[here, :] = value
            else:
                for j in range(block // width):
                    stage[m * (block // width) + j] = value[j * width:(j + 1) * width, :]

        each(0, window // block, multiply)

    def part_copy(k):
        peer = lax.rem(me + k, owners)
        return pltpu.make_async_remote_copy(
            src_ref=stage.at[peer],
            dst_ref=parts.at[k],
            send_sem=part_send.at[k],
            recv_sem=part_recv.at[k],
            device_id={"dp": peer},
        )

    each(1, owners, lambda k: part_copy(k).start())

    steps = jnp.full((1, columns), step[0], jnp.int32).astype(F32)
    corr_one = 1.0 - jnp.exp(steps * math.log(0.9))
    corr_two = 1.0 - jnp.exp(steps * math.log(0.95))
    for copy in state_copies:
        copy.wait()

    acc_own = acc.at[pl.ds(0, width), :]
    acc_own[...] = stage[me]

    def take(k):
        part_copy(k).wait_recv()
        acc_own[...] += parts[k]

    each(1, owners, take)
    owned = acc_own[...]
    master = state[0]
    new_first = 0.9 * state[1] + 0.1 * owned
    new_second = 0.95 * state[2] + 0.05 * owned * owned
    update = new_first / corr_one / (jnp.sqrt(new_second / corr_two) + 1e-08)
    new_master = master - 0.01 * (update + 0.01 * master)
    packed = jnp.concatenate(
        [new_master[:, g * span:(g + 1) * span] for g in range(groups)], axis=0
    )
    rows[me] = packed.astype(BF16)

    def row_copy(k):
        return pltpu.make_async_remote_copy(
            src_ref=rows.at[me],
            dst_ref=rows.at[me],
            send_sem=row_send.at[k],
            recv_sem=row_recv.at[k],
            device_id={"dp": lax.rem(me + k, owners)},
        )

    def row_arrival(k):
        source = lax.rem(me + owners - k, owners)
        return pltpu.make_async_remote_copy(
            src_ref=rows.at[source],
            dst_ref=rows.at[source],
            send_sem=row_send.at[k],
            recv_sem=row_recv.at[k],
            device_id={"dp": source},
        )

    each(1, owners, lambda k: row_copy(k).start())
    fresh[0] = new_master
    fresh[1] = new_first
    fresh[2] = new_second
    out_copies = [
        pltpu.make_async_copy(fresh.at[i], target.at[0], out_sem.at[i])
        for i, target in enumerate((out_master, out_first, out_second))
    ]
    for copy in out_copies:
        copy.start()

    each(1, owners, lambda k: row_arrival(k).wait_recv())

    def assemble(q):
        blocks = [rows[table[q * groups + j]].astype(F32) for j in range(groups)]
        for g in range(groups):
            piece = jnp.concatenate(
                [b[g * width:(g + 1) * width, :] for b in blocks], axis=0
            )
            weight[pl.ds(pl.multiple_of(q * groups * width, 16), groups * width),
                   g * span:(g + 1) * span] = piece.astype(BF16)

    each(0, buckets // groups, assemble)
    weight_copy = pltpu.make_async_copy(weight, out_weight, out_sem.at[3])
    weight_copy.start()

    for k in range(1, ranks):
        og_copy(k).wait_send()
    each(1, owners, lambda k: part_copy(k).wait_send())
    each(1, owners, lambda k: row_copy(k).wait_send())
    for copy in out_copies:
        copy.wait()
    weight_copy.wait()


def shards(owners, ranks, context, out_grad, owner_table, step_count, master, first, second):
    buckets = owner_table.shape[0]
    width = master.shape[1]
    tokens, window = out_grad.shape
    columns = context.shape[1]
    groups = 16 // width
    state_shape = jax.ShapeDtypeStruct(master.shape, F32)
    hbm = pl.BlockSpec(memory_space=pltpu.HBM)
    smem = pl.BlockSpec(memory_space=pltpu.SMEM)
    dma = pltpu.SemaphoreType.DMA
    return pl.pallas_call(
        functools.partial(kernel, owners, ranks, buckets, width),
        out_shape=(
            state_shape,
            state_shape,
            state_shape,
            jax.ShapeDtypeStruct((window, columns), BF16),
        ),
        in_specs=[smem, smem] + [hbm] * 5,
        out_specs=(hbm,) * 4,
        scratch_shapes=[
            pltpu.VMEM((window, tokens), BF16),
            pltpu.VMEM((ranks, window, tokens), BF16),
            pltpu.VMEM((ranks, tokens, columns), BF16),
            pltpu.VMEM((window, columns), F32),
            pltpu.VMEM((owners, width, columns), F32),
            pltpu.VMEM((owners, width, columns), F32),
            pltpu.VMEM((3, width, columns), F32),
            pltpu.VMEM((3, width, columns), F32),
            pltpu.VMEM((owners, groups * width, columns // groups), BF16),
            pltpu.VMEM((window, columns), BF16),
            dma, dma((ranks,)), dma((3,)), dma((4,)),
            dma((ranks,)), dma((ranks,)),
            dma((owners,)), dma((owners,)),
            dma((owners,)), dma((owners,)),
        ],
        compiler_params=pltpu.CompilerParams(
            collective_id=0, has_side_effects=True, vmem_limit_bytes=40 * 1024 * 1024
        ),
        cost_estimate=pl.CostEstimate(
            flops=2 * window * columns * tokens * ranks,
            bytes_accessed=2 * ranks * tokens * columns,
            transcendentals=0,
        ),
    )(owner_table, step_count, out_grad.T, context, master, first, second)


def solution(mesh):
    placed = (
        P("dp", "tensor"),
        P(("dp", "tensor"), None),
        P(),
        P(),
        P("dp", None, "tensor"),
        P("dp", None, "tensor"),
        P("dp", None, "tensor"),
    )
    return jax.shard_map(
        functools.partial(shards, mesh.shape["dp"], mesh.shape["tensor"]),
        mesh=mesh,
        in_specs=placed,
        out_specs=(
            P("dp", None, "tensor"),
            P("dp", None, "tensor"),
            P("dp", None, "tensor"),
            P(None, "tensor"),
        ),
        check_vma=False,
    )
```

```python
import functools
import math

import jax
import jax.numpy as jnp
from jax import lax
from jax.experimental import pallas as pl
from jax.experimental.pallas import tpu as pltpu
from jax.sharding import PartitionSpec as P

F32 = jnp.float32
BF16 = jnp.bfloat16


def each(low, high, body):
    if high - low <= 16:
        for at in range(low, high):
            body(at)
    else:
        lax.fori_loop(low, high, lambda at, none: (body(at), none)[1], None)


def kernel(
    owners, ranks, buckets, width,
    table_hbm, step, og_hbm, ctx_hbm, master_hbm, first_hbm, second_hbm,
    out_master, out_first, out_second, rows,
    table, table_sem, og_all, ctx, acc, product, stage, parts, state,
    og_own_sem, ctx_sem, state_sem,
    og_send, og_recv, part_send, part_recv, row_send, row_recv,
):
    me = lax.axis_index("dp")
    rank = lax.axis_index("tensor")
    window, tokens = og_hbm.shape
    columns = ctx.shape[2]
    groups = rows.shape[1] // width
    span = columns // groups

    barrier = pltpu.get_barrier_semaphore()

    def greet_rank(k):
        pl.semaphore_signal(barrier, inc=1, device_id={"tensor": lax.rem(rank + k, ranks)})

    def greet_owner(k):
        pl.semaphore_signal(barrier, inc=1, device_id={"dp": lax.rem(me + k, owners)})

    each(1, ranks, greet_rank)
    each(1, owners, greet_owner)

    table_copy = pltpu.make_async_copy(table_hbm, table, table_sem)
    table_copy.start()
    own_copy = pltpu.make_async_copy(og_hbm, og_all.at[rank], og_own_sem)
    own_copy.start()

    def ctx_copy(k):
        at = lax.rem(rank + k, ranks)
        first = pl.multiple_of(at * tokens, 16)
        return pltpu.make_async_copy(
            ctx_hbm.at[pl.ds(first, tokens), :], ctx.at[at], ctx_sem.at[at]
        )

    for k in range(ranks):
        ctx_copy(k).start()
    state_copies = [
        pltpu.make_async_copy(source.at[0], state.at[i], state_sem.at[i])
        for i, source in enumerate((master_hbm, first_hbm, second_hbm))
    ]
    for copy in state_copies:
        copy.start()

    def bucket_of(r):
        def check(b, found):
            return jnp.where(table[b] == r, b, found)

        if buckets > 16:
            return lax.fori_loop(0, buckets, check, 0)
        found = 0
        for b in range(buckets):
            found = check(b, found)
        return found

    table_copy.wait()
    ready = [bucket_of(r) for r in range(buckets)] if buckets <= 16 else None

    own_copy.wait()
    pl.semaphore_wait(barrier, ranks + owners - 2)

    def og_copy(k):
        peer = lax.rem(rank + k, ranks)
        return pltpu.make_async_remote_copy(
            src_ref=og_all.at[rank],
            dst_ref=og_all.at[rank],
            send_sem=og_send.at[k],
            recv_sem=og_recv.at[k],
            device_id={"tensor": peer},
        )

    def og_arrival(k):
        source = lax.rem(rank + ranks - k, ranks)
        return pltpu.make_async_remote_copy(
            src_ref=og_all.at[source],
            dst_ref=og_all.at[source],
            send_sem=og_send.at[k],
            recv_sem=og_recv.at[k],
            device_id={"tensor": source},
        )

    for k in range(1, ranks):
        og_copy(k).start()

    block = min(window, 8 * width)
    for i in range(ranks):
        at = lax.rem(rank + ranks - i, ranks)
        if i:
            og_arrival(i).wait_recv()
        ctx_copy((ranks - i) % ranks).wait()

        def multiply(m, i=i, at=at):
            here = pl.ds(m * block, block)
            value = jnp.dot(og_all[at, here, :], ctx[at], preferred_element_type=F32)
            if i:
                value = acc[here, :] + value
            if i < ranks - 1:
                acc[here, :] = value
            else:
                for j in range(block // width):
                    product[m * (block // width) + j] = value[j * width:(j + 1) * width, :]

        each(0, window // block, multiply)

    def place(r):
        stage[r] = product[ready[r] if ready else bucket_of(r)]

    each(0, buckets, place)

    def part_copy(k):
        peer = lax.rem(me + k, owners)
        return pltpu.make_async_remote_copy(
            src_ref=stage.at[peer],
            dst_ref=parts.at[k],
            send_sem=part_send.at[k],
            recv_sem=part_recv.at[k],
            device_id={"dp": peer},
        )

    each(1, owners, lambda k: part_copy(k).start())

    steps = jnp.full((1, columns), step[0], jnp.int32).astype(F32)
    corr_one = 1.0 - jnp.exp(steps * math.log(0.9))
    corr_two = 1.0 - jnp.exp(steps * math.log(0.95))
    for copy in state_copies:
        copy.wait()

    acc_own = acc.at[pl.ds(0, width), :]
    acc_own[...] = stage[me]

    def take(k):
        part_copy(k).wait_recv()
        acc_own[...] += parts[k]

    each(1, owners, take)
    owned = acc_own[...]
    master = state[0]
    new_first = 0.9 * state[1] + 0.1 * owned
    new_second = 0.95 * state[2] + 0.05 * owned * owned
    update = new_first / corr_one / (jnp.sqrt(new_second / corr_two) + 1e-08)
    new_master = master - 0.01 * (update + 0.01 * master)
    joined = jnp.concatenate(
        [new_master[:, g * span:(g + 1) * span] for g in range(groups)], axis=0
    )
    rows[me] = joined.astype(BF16)

    def row_copy(k):
        return pltpu.make_async_remote_copy(
            src_ref=rows.at[me],
            dst_ref=rows.at[me],
            send_sem=row_send.at[k],
            recv_sem=row_recv.at[k],
            device_id={"dp": lax.rem(me + k, owners)},
        )

    def row_arrival(k):
        source = lax.rem(me + owners - k, owners)
        return pltpu.make_async_remote_copy(
            src_ref=rows.at[source],
            dst_ref=rows.at[source],
            send_sem=row_send.at[k],
            recv_sem=row_recv.at[k],
            device_id={"dp": source},
        )

    each(1, owners, lambda k: row_copy(k).start())
    out_master[0] = new_master
    out_first[0] = new_first
    out_second[0] = new_second

    each(1, owners, lambda k: row_arrival(k).wait_recv())

    for k in range(1, ranks):
        og_copy(k).wait_send()
    each(1, owners, lambda k: part_copy(k).wait_send())
    each(1, owners, lambda k: row_copy(k).wait_send())


def finish_kernel(
    buckets, width, table, master, first, second, rows,
    out_master, out_first, out_second, out_weight, weight, out_sem,
):
    groups = rows.shape[1] // width
    span = rows.shape[2]
    copies = [
        pltpu.make_async_copy(source, target, out_sem.at[i])
        for i, (source, target) in enumerate(
            ((master, out_master), (first, out_first), (second, out_second))
        )
    ]
    for copy in copies:
        copy.start()

    def assemble(q):
        blocks = [rows[table[q * groups + j]].astype(F32) for j in range(groups)]
        for g in range(groups):
            piece = jnp.concatenate(
                [b[g * width:(g + 1) * width, :] for b in blocks], axis=0
            )
            here = pl.ds(pl.multiple_of(q * groups * width, 16), groups * width)
            weight[here, g * span:(g + 1) * span] = piece.astype(BF16)

    each(0, buckets // groups, assemble)
    weight_copy = pltpu.make_async_copy(weight, out_weight, out_sem.at[3])
    weight_copy.start()
    for copy in copies:
        copy.wait()
    weight_copy.wait()


def shards(owners, ranks, context, out_grad, owner_table, step_count, master, first, second):
    buckets = owner_table.shape[0]
    width = master.shape[1]
    tokens, window = out_grad.shape
    columns = context.shape[1]
    groups = 16 // width
    state_shape = jax.ShapeDtypeStruct(master.shape, F32)
    hbm = pl.BlockSpec(memory_space=pltpu.HBM)
    smem = pl.BlockSpec(memory_space=pltpu.SMEM)
    dma = pltpu.SemaphoreType.DMA
    weight_shape = jax.ShapeDtypeStruct((window, columns), BF16)
    new_master, new_first, new_second, rows = pl.pallas_call(
        functools.partial(kernel, owners, ranks, buckets, width),
        out_shape=(
            pltpu.VMEM(master.shape, F32),
            pltpu.VMEM(master.shape, F32),
            pltpu.VMEM(master.shape, F32),
            pltpu.VMEM((owners, groups * width, columns // groups), BF16),
        ),
        in_specs=[hbm, smem] + [hbm] * 5,
        out_specs=(pl.BlockSpec(memory_space=pltpu.VMEM),) * 4,
        scratch_shapes=[
            pltpu.SMEM((buckets,), jnp.int32),
            dma,
            pltpu.VMEM((ranks, window, tokens), BF16),
            pltpu.VMEM((ranks, tokens, columns), BF16),
            pltpu.VMEM((window, columns), F32),
            pltpu.VMEM((buckets, width, columns), F32),
            pltpu.VMEM((owners, width, columns), F32),
            pltpu.VMEM((owners, width, columns), F32),
            pltpu.VMEM((3, width, columns), F32),
            dma, dma((ranks,)), dma((3,)),
            dma((ranks,)), dma((ranks,)),
            dma((owners,)), dma((owners,)),
            dma((owners,)), dma((owners,)),
        ],
        compiler_params=pltpu.CompilerParams(
            collective_id=0, has_side_effects=True, vmem_limit_bytes=56 * 1024 * 1024
        ),
        cost_estimate=pl.CostEstimate(
            flops=2 * window * columns * tokens * ranks,
            bytes_accessed=2 * ranks * tokens * columns,
            transcendentals=0,
        ),
    )(owner_table, step_count, out_grad.T, context, master, first, second)
    return pl.pallas_call(
        functools.partial(finish_kernel, buckets, width),
        out_shape=(state_shape, state_shape, state_shape, weight_shape),
        in_specs=[smem] + [hbm] * 3 + [pl.BlockSpec(memory_space=pltpu.VMEM)],
        out_specs=(hbm,) * 4,
        scratch_shapes=[pltpu.VMEM((window, columns), BF16), dma((4,))],
        compiler_params=pltpu.CompilerParams(vmem_limit_bytes=16 * 1024 * 1024),
    )(owner_table, new_master, new_first, new_second, rows)


def solution(mesh):
    placed = (
        P("dp", "tensor"),
        P(("dp", "tensor"), None),
        P(),
        P(),
        P("dp", None, "tensor"),
        P("dp", None, "tensor"),
        P("dp", None, "tensor"),
    )
    return jax.shard_map(
        functools.partial(shards, mesh.shape["dp"], mesh.shape["tensor"]),
        mesh=mesh,
        in_specs=placed,
        out_specs=(
            P("dp", None, "tensor"),
            P("dp", None, "tensor"),
            P("dp", None, "tensor"),
            P(None, "tensor"),
        ),
        check_vma=False,
    )
```

```python
import functools
import math

import jax
import jax.numpy as jnp
from jax import lax
from jax.experimental import pallas as pl
from jax.experimental.pallas import tpu as pltpu
from jax.sharding import PartitionSpec as P

F32 = jnp.float32
BF16 = jnp.bfloat16


def each(low, high, body):
    if high - low <= 16:
        for at in range(low, high):
            body(at)
    else:
        lax.fori_loop(low, high, lambda at, none: (body(at), none)[1], None)


def flipped(at, k, size):
    total, bit = 0, 1
    while bit < size:
        total = total + (at // bit + k // bit) % 2 * bit
        bit *= 2
    return total


def kernel(
    owners, ranks, buckets, width,
    table_hbm, step, og_hbm, ctx_hbm, master_hbm, first_hbm, second_hbm,
    out_master, out_first, out_second, rows,
    table, table_sem, og_all, ctx, acc, product, stage, parts, state,
    og_own_sem, ctx_sem, state_sem,
    og_send, og_recv, part_send, part_recv, row_send, row_recv,
):
    me = lax.axis_index("dp")
    rank = lax.axis_index("tensor")
    window, tokens = og_hbm.shape
    columns = ctx.shape[2]
    groups = rows.shape[1] // width
    span = columns // groups

    barrier = pltpu.get_barrier_semaphore()

    def greet_rank(k):
        pl.semaphore_signal(barrier, inc=1, device_id={"tensor": flipped(rank, k, ranks)})

    def greet_owner(k):
        pl.semaphore_signal(barrier, inc=1, device_id={"dp": flipped(me, k, owners)})

    each(1, ranks, lambda k: greet_rank(ranks - k))
    each(1, owners, greet_owner)

    table_copy = pltpu.make_async_copy(table_hbm, table, table_sem)
    table_copy.start()
    own_copy = pltpu.make_async_copy(og_hbm, og_all.at[rank], og_own_sem)
    own_copy.start()

    def ctx_copy(k):
        at = flipped(rank, k, ranks)
        first = pl.multiple_of(at * tokens, 16)
        return pltpu.make_async_copy(
            ctx_hbm.at[pl.ds(first, tokens), :], ctx.at[at], ctx_sem.at[at]
        )

    for k in range(ranks):
        ctx_copy(k).start()
    state_copies = [
        pltpu.make_async_copy(source.at[0], state.at[i], state_sem.at[i])
        for i, source in enumerate((master_hbm, first_hbm, second_hbm))
    ]
    for copy in state_copies:
        copy.start()

    def bucket_of(r):
        def check(b, found):
            return jnp.where(table[b] == r, b, found)

        if buckets > 16:
            return lax.fori_loop(0, buckets, check, 0)
        found = 0
        for b in range(buckets):
            found = check(b, found)
        return found

    table_copy.wait()
    ready = [bucket_of(r) for r in range(buckets)] if buckets <= 16 else None

    own_copy.wait()
    pl.semaphore_wait(barrier, ranks + owners - 2)

    def og_copy(k):
        peer = flipped(rank, k, ranks)
        return pltpu.make_async_remote_copy(
            src_ref=og_all.at[rank],
            dst_ref=og_all.at[rank],
            send_sem=og_send.at[k],
            recv_sem=og_recv.at[k],
            device_id={"tensor": peer},
        )

    def og_arrival(k):
        source = flipped(rank, k, ranks)
        return pltpu.make_async_remote_copy(
            src_ref=og_all.at[source],
            dst_ref=og_all.at[source],
            send_sem=og_send.at[k],
            recv_sem=og_recv.at[k],
            device_id={"tensor": source},
        )

    for k in range(ranks - 1, 0, -1):
        og_copy(k).start()

    block = min(window, 8 * width)
    for i in range(ranks):
        at = flipped(rank, i, ranks)
        if i:
            og_arrival(i).wait_recv()
        ctx_copy(i).wait()

        def multiply(m, i=i, at=at):
            here = pl.ds(m * block, block)
            value = jnp.dot(og_all[at, here, :], ctx[at], preferred_element_type=F32)
            if i:
                value = acc[here, :] + value
            if i < ranks - 1:
                acc[here, :] = value
            else:
                for j in range(block // width):
                    product[m * (block // width) + j] = value[j * width:(j + 1) * width, :]

        each(0, window // block, multiply)

    def place(r):
        stage[r] = product[ready[r] if ready else bucket_of(r)]

    each(0, buckets, place)

    def part_copy(k):
        peer = flipped(me, k, owners)
        return pltpu.make_async_remote_copy(
            src_ref=stage.at[peer],
            dst_ref=parts.at[k],
            send_sem=part_send.at[k],
            recv_sem=part_recv.at[k],
            device_id={"dp": peer},
        )

    each(1, owners, lambda k: part_copy(owners - k).start())

    steps = jnp.full((1, columns), step[0], jnp.int32).astype(F32)
    corr_one = 1.0 - jnp.exp(steps * math.log(0.9))
    corr_two = 1.0 - jnp.exp(steps * math.log(0.95))
    for copy in state_copies:
        copy.wait()

    acc_own = acc.at[pl.ds(0, width), :]
    acc_own[...] = stage[me]

    def take(k):
        part_copy(k).wait_recv()
        acc_own[...] += parts[k]

    each(1, owners, take)
    owned = acc_own[...]
    master = state[0]
    new_first = 0.9 * state[1] + 0.1 * owned
    new_second = 0.95 * state[2] + 0.05 * owned * owned
    update = new_first / corr_one / (jnp.sqrt(new_second / corr_two) + 1e-08)
    new_master = master - 0.01 * (update + 0.01 * master)
    joined = jnp.concatenate(
        [new_master[:, g * span:(g + 1) * span] for g in range(groups)], axis=0
    )
    rows[me] = joined.astype(BF16)

    def row_copy(k):
        return pltpu.make_async_remote_copy(
            src_ref=rows.at[me],
            dst_ref=rows.at[me],
            send_sem=row_send.at[k],
            recv_sem=row_recv.at[k],
            device_id={"dp": flipped(me, k, owners)},
        )

    def row_arrival(k):
        source = flipped(me, k, owners)
        return pltpu.make_async_remote_copy(
            src_ref=rows.at[source],
            dst_ref=rows.at[source],
            send_sem=row_send.at[k],
            recv_sem=row_recv.at[k],
            device_id={"dp": source},
        )

    each(1, owners, lambda k: row_copy(owners - k).start())
    out_master[0] = new_master
    out_first[0] = new_first
    out_second[0] = new_second

    each(1, owners, lambda k: row_arrival(k).wait_recv())

    for k in range(1, ranks):
        og_copy(k).wait_send()
    each(1, owners, lambda k: part_copy(k).wait_send())
    each(1, owners, lambda k: row_copy(k).wait_send())


def finish_kernel(
    buckets, width, table, master, first, second, rows,
    out_master, out_first, out_second, out_weight, weight, out_sem,
):
    groups = rows.shape[1] // width
    span = rows.shape[2]
    copies = [
        pltpu.make_async_copy(source, target, out_sem.at[i])
        for i, (source, target) in enumerate(
            ((master, out_master), (first, out_first), (second, out_second))
        )
    ]
    for copy in copies:
        copy.start()

    def assemble(q):
        blocks = [rows[table[q * groups + j]].astype(F32) for j in range(groups)]
        for g in range(groups):
            piece = jnp.concatenate(
                [b[g * width:(g + 1) * width, :] for b in blocks], axis=0
            )
            here = pl.ds(pl.multiple_of(q * groups * width, 16), groups * width)
            weight[here, g * span:(g + 1) * span] = piece.astype(BF16)

    each(0, buckets // groups, assemble)
    weight_copy = pltpu.make_async_copy(weight, out_weight, out_sem.at[3])
    weight_copy.start()
    for copy in copies:
        copy.wait()
    weight_copy.wait()


def shards(owners, ranks, context, out_grad, owner_table, step_count, master, first, second):
    buckets = owner_table.shape[0]
    width = master.shape[1]
    tokens, window = out_grad.shape
    columns = context.shape[1]
    groups = 16 // width
    state_shape = jax.ShapeDtypeStruct(master.shape, F32)
    hbm = pl.BlockSpec(memory_space=pltpu.HBM)
    smem = pl.BlockSpec(memory_space=pltpu.SMEM)
    dma = pltpu.SemaphoreType.DMA
    weight_shape = jax.ShapeDtypeStruct((window, columns), BF16)
    new_master, new_first, new_second, rows = pl.pallas_call(
        functools.partial(kernel, owners, ranks, buckets, width),
        out_shape=(
            pltpu.VMEM(master.shape, F32),
            pltpu.VMEM(master.shape, F32),
            pltpu.VMEM(master.shape, F32),
            pltpu.VMEM((owners, groups * width, columns // groups), BF16),
        ),
        in_specs=[hbm, smem] + [hbm] * 5,
        out_specs=(pl.BlockSpec(memory_space=pltpu.VMEM),) * 4,
        scratch_shapes=[
            pltpu.SMEM((buckets,), jnp.int32),
            dma,
            pltpu.VMEM((ranks, window, tokens), BF16),
            pltpu.VMEM((ranks, tokens, columns), BF16),
            pltpu.VMEM((window, columns), F32),
            pltpu.VMEM((buckets, width, columns), F32),
            pltpu.VMEM((owners, width, columns), F32),
            pltpu.VMEM((owners, width, columns), F32),
            pltpu.VMEM((3, width, columns), F32),
            dma, dma((ranks,)), dma((3,)),
            dma((ranks,)), dma((ranks,)),
            dma((owners,)), dma((owners,)),
            dma((owners,)), dma((owners,)),
        ],
        compiler_params=pltpu.CompilerParams(
            collective_id=0, has_side_effects=True, vmem_limit_bytes=56 * 1024 * 1024
        ),
        cost_estimate=pl.CostEstimate(
            flops=2 * window * columns * tokens * ranks,
            bytes_accessed=2 * ranks * tokens * columns,
            transcendentals=0,
        ),
    )(owner_table, step_count, out_grad.T, context, master, first, second)
    return pl.pallas_call(
        functools.partial(finish_kernel, buckets, width),
        out_shape=(state_shape, state_shape, state_shape, weight_shape),
        in_specs=[smem] + [hbm] * 3 + [pl.BlockSpec(memory_space=pltpu.VMEM)],
        out_specs=(hbm,) * 4,
        scratch_shapes=[pltpu.VMEM((window, columns), BF16), dma((4,))],
        compiler_params=pltpu.CompilerParams(vmem_limit_bytes=16 * 1024 * 1024),
    )(owner_table, new_master, new_first, new_second, rows)


def solution(mesh):
    placed = (
        P("dp", "tensor"),
        P(("dp", "tensor"), None),
        P(),
        P(),
        P("dp", None, "tensor"),
        P("dp", None, "tensor"),
        P("dp", None, "tensor"),
    )
    return jax.shard_map(
        functools.partial(shards, mesh.shape["dp"], mesh.shape["tensor"]),
        mesh=mesh,
        in_specs=placed,
        out_specs=(
            P("dp", None, "tensor"),
            P("dp", None, "tensor"),
            P("dp", None, "tensor"),
            P(None, "tensor"),
        ),
        check_vma=False,
    )
```

```python
import functools
import math

import jax
import jax.numpy as jnp
from jax import lax
from jax.experimental import pallas as pl
from jax.experimental.pallas import tpu as pltpu
from jax.sharding import PartitionSpec as P

F32 = jnp.float32
BF16 = jnp.bfloat16


def each(low, high, body):
    if high - low <= 16:
        for at in range(low, high):
            body(at)
    else:
        lax.fori_loop(low, high, lambda at, none: (body(at), none)[1], None)


def flipped(at, k, size):
    total, bit = 0, 1
    while bit < size:
        total = total + (at // bit + k // bit) % 2 * bit
        bit *= 2
    return total


def kernel(
    owners, ranks, buckets, width,
    table_hbm, step, og_hbm, ctx_hbm, master_hbm, first_hbm, second_hbm,
    out_master, out_first, out_second, rows,
    table, table_sem, og_all, ctx, acc, product, stage, parts, state,
    og_own_sem, ctx_sem, state_sem,
    og_send, og_recv, part_send, part_recv, row_send, row_recv,
):
    me = lax.axis_index("dp")
    rank = lax.axis_index("tensor")
    window, tokens = og_hbm.shape
    columns = ctx.shape[2]
    groups = rows.shape[1] // width
    span = columns // groups

    barrier = pltpu.get_barrier_semaphore()

    def greet_rank(k):
        pl.semaphore_signal(barrier, inc=1, device_id={"tensor": flipped(rank, k, ranks)})

    def greet_owner(k):
        pl.semaphore_signal(barrier, inc=1, device_id={"dp": flipped(me, k, owners)})

    each(1, ranks, lambda k: greet_rank(ranks - k))
    each(1, owners, lambda k: greet_owner(owners - k))

    table_copy = pltpu.make_async_copy(table_hbm, table, table_sem)
    table_copy.start()
    own_copy = pltpu.make_async_copy(og_hbm, og_all.at[rank], og_own_sem)
    own_copy.start()

    def ctx_copy(k):
        at = flipped(rank, k, ranks)
        first = pl.multiple_of(at * tokens, 16)
        return pltpu.make_async_copy(
            ctx_hbm.at[pl.ds(first, tokens), :], ctx.at[at], ctx_sem.at[at]
        )

    for k in range(ranks):
        ctx_copy(k).start()
    state_copies = [
        pltpu.make_async_copy(source.at[0], state.at[i], state_sem.at[i])
        for i, source in enumerate((master_hbm, first_hbm, second_hbm))
    ]
    for copy in state_copies:
        copy.start()

    def bucket_of(r):
        def check(b, found):
            return jnp.where(table[b] == r, b, found)

        if buckets > 16:
            return lax.fori_loop(0, buckets, check, 0)
        found = 0
        for b in range(buckets):
            found = check(b, found)
        return found

    table_copy.wait()
    ready = [bucket_of(r) for r in range(buckets)] if buckets <= 16 else None

    own_copy.wait()
    pl.semaphore_wait(barrier, ranks + owners - 2)

    def og_copy(k):
        peer = flipped(rank, k, ranks)
        return pltpu.make_async_remote_copy(
            src_ref=og_all.at[rank],
            dst_ref=og_all.at[rank],
            send_sem=og_send.at[k],
            recv_sem=og_recv.at[k],
            device_id={"tensor": peer},
        )

    def og_arrival(k):
        source = flipped(rank, k, ranks)
        return pltpu.make_async_remote_copy(
            src_ref=og_all.at[source],
            dst_ref=og_all.at[source],
            send_sem=og_send.at[k],
            recv_sem=og_recv.at[k],
            device_id={"tensor": source},
        )

    for k in range(ranks - 1, 0, -1):
        og_copy(k).start()

    block = min(window, 8 * width)
    for i in range(ranks):
        at = flipped(rank, i, ranks)
        if i:
            og_arrival(i).wait_recv()
        ctx_copy(i).wait()

        def multiply(m, i=i, at=at):
            here = pl.ds(m * block, block)
            value = jnp.dot(og_all[at, here, :], ctx[at], preferred_element_type=F32)
            if i:
                value = acc[here, :] + value
            if i < ranks - 1:
                acc[here, :] = value
            else:
                for j in range(block // width):
                    product[m * (block // width) + j] = value[j * width:(j + 1) * width, :]

        each(0, window // block, multiply)

    def place(r):
        stage[r] = product[ready[r] if ready else bucket_of(r)]

    each(0, buckets, place)

    def part_copy(k):
        peer = flipped(me, k, owners)
        return pltpu.make_async_remote_copy(
            src_ref=stage.at[peer],
            dst_ref=parts.at[k],
            send_sem=part_send.at[k],
            recv_sem=part_recv.at[k],
            device_id={"dp": peer},
        )

    each(1, owners, lambda k: part_copy(owners - k).start())

    steps = jnp.full((1, columns), step[0], jnp.int32).astype(F32)
    corr_one = 1.0 - jnp.exp(steps * math.log(0.9))
    corr_two = 1.0 - jnp.exp(steps * math.log(0.95))
    for copy in state_copies:
        copy.wait()

    acc_own = acc.at[pl.ds(0, width), :]
    acc_own[...] = stage[me]

    def take(k):
        part_copy(k).wait_recv()
        acc_own[...] += parts[k]

    each(1, owners, take)
    owned = acc_own[...]
    master = state[0]
    new_first = 0.9 * state[1] + 0.1 * owned
    new_second = 0.95 * state[2] + 0.05 * owned * owned
    update = new_first / corr_one / (jnp.sqrt(new_second / corr_two) + 1e-08)
    new_master = master - 0.01 * (update + 0.01 * master)
    joined = jnp.concatenate(
        [new_master[:, g * span:(g + 1) * span] for g in range(groups)], axis=0
    )
    rows[me] = joined.astype(BF16)

    def row_copy(k):
        return pltpu.make_async_remote_copy(
            src_ref=rows.at[me],
            dst_ref=rows.at[me],
            send_sem=row_send.at[k],
            recv_sem=row_recv.at[k],
            device_id={"dp": flipped(me, k, owners)},
        )

    def row_arrival(k):
        source = flipped(me, k, owners)
        return pltpu.make_async_remote_copy(
            src_ref=rows.at[source],
            dst_ref=rows.at[source],
            send_sem=row_send.at[k],
            recv_sem=row_recv.at[k],
            device_id={"dp": source},
        )

    each(1, owners, lambda k: row_copy(owners - k).start())
    out_master[0] = new_master
    out_first[0] = new_first
    out_second[0] = new_second

    each(1, owners, lambda k: row_arrival(k).wait_recv())

    for k in range(1, ranks):
        og_copy(k).wait_send()
    each(1, owners, lambda k: part_copy(k).wait_send())
    each(1, owners, lambda k: row_copy(k).wait_send())


def finish_kernel(
    buckets, width, table, master, first, second, rows,
    out_master, out_first, out_second, out_weight, weight, out_sem,
):
    groups = rows.shape[1] // width
    span = rows.shape[2]
    copies = [
        pltpu.make_async_copy(source, target, out_sem.at[i])
        for i, (source, target) in enumerate(
            ((master, out_master), (first, out_first), (second, out_second))
        )
    ]
    for copy in copies:
        copy.start()

    def assemble(q):
        blocks = [rows[table[q * groups + j]].astype(F32) for j in range(groups)]
        for g in range(groups):
            piece = jnp.concatenate(
                [b[g * width:(g + 1) * width, :] for b in blocks], axis=0
            )
            here = pl.ds(pl.multiple_of(q * groups * width, 16), groups * width)
            weight[here, g * span:(g + 1) * span] = piece.astype(BF16)

    each(0, buckets // groups, assemble)
    weight_copy = pltpu.make_async_copy(weight, out_weight, out_sem.at[3])
    weight_copy.start()
    for copy in copies:
        copy.wait()
    weight_copy.wait()


def shards(owners, ranks, context, out_grad, owner_table, step_count, master, first, second):
    buckets = owner_table.shape[0]
    width = master.shape[1]
    tokens, window = out_grad.shape
    columns = context.shape[1]
    groups = 16 // width
    state_shape = jax.ShapeDtypeStruct(master.shape, F32)
    hbm = pl.BlockSpec(memory_space=pltpu.HBM)
    smem = pl.BlockSpec(memory_space=pltpu.SMEM)
    dma = pltpu.SemaphoreType.DMA
    weight_shape = jax.ShapeDtypeStruct((window, columns), BF16)
    new_master, new_first, new_second, rows = pl.pallas_call(
        functools.partial(kernel, owners, ranks, buckets, width),
        out_shape=(
            pltpu.VMEM(master.shape, F32),
            pltpu.VMEM(master.shape, F32),
            pltpu.VMEM(master.shape, F32),
            pltpu.VMEM((owners, groups * width, columns // groups), BF16),
        ),
        in_specs=[hbm, smem] + [hbm] * 5,
        out_specs=(pl.BlockSpec(memory_space=pltpu.VMEM),) * 4,
        scratch_shapes=[
            pltpu.SMEM((buckets,), jnp.int32),
            dma,
            pltpu.VMEM((ranks, window, tokens), BF16),
            pltpu.VMEM((ranks, tokens, columns), BF16),
            pltpu.VMEM((window, columns), F32),
            pltpu.VMEM((buckets, width, columns), F32),
            pltpu.VMEM((owners, width, columns), F32),
            pltpu.VMEM((owners, width, columns), F32),
            pltpu.VMEM((3, width, columns), F32),
            dma, dma((ranks,)), dma((3,)),
            dma((ranks,)), dma((ranks,)),
            dma((owners,)), dma((owners,)),
            dma((owners,)), dma((owners,)),
        ],
        compiler_params=pltpu.CompilerParams(
            collective_id=0, has_side_effects=True, vmem_limit_bytes=56 * 1024 * 1024
        ),
        cost_estimate=pl.CostEstimate(
            flops=2 * window * columns * tokens * ranks,
            bytes_accessed=2 * ranks * tokens * columns,
            transcendentals=0,
        ),
    )(owner_table, step_count, out_grad.T, context, master, first, second)
    return pl.pallas_call(
        functools.partial(finish_kernel, buckets, width),
        out_shape=(state_shape, state_shape, state_shape, weight_shape),
        in_specs=[smem] + [hbm] * 3 + [pl.BlockSpec(memory_space=pltpu.VMEM)],
        out_specs=(hbm,) * 4,
        scratch_shapes=[pltpu.VMEM((window, columns), BF16), dma((4,))],
        compiler_params=pltpu.CompilerParams(vmem_limit_bytes=16 * 1024 * 1024),
    )(owner_table, new_master, new_first, new_second, rows)


def solution(mesh):
    placed = (
        P("dp", "tensor"),
        P(("dp", "tensor"), None),
        P(),
        P(),
        P("dp", None, "tensor"),
        P("dp", None, "tensor"),
        P("dp", None, "tensor"),
    )
    return jax.shard_map(
        functools.partial(shards, mesh.shape["dp"], mesh.shape["tensor"]),
        mesh=mesh,
        in_specs=placed,
        out_specs=(
            P("dp", None, "tensor"),
            P("dp", None, "tensor"),
            P("dp", None, "tensor"),
            P(None, "tensor"),
        ),
        check_vma=False,
    )
```
